256 devices in a mesh: row: 8 (over z), col: 4 (over x_hi, core), dep: 8 (over x_lo, y).
Axes of the slice: x: 4 (x_hi: 2, x_lo: 2; x = x_hi * 2 + x_lo), y: 4, z: 8, core: 2. Of those that a mesh axis runs over, the one named last changes fastest.
Arguments:
- tokens: bfloat16 [1024, 12288], P(('row', 'col'), 'dep'), may hold values from -16 to 16
- w_up: bfloat16 [12288, 49152], P('dep', ('row', 'col')), may hold values from -0.14433757 to 0.14433757
- bias_up: float32 [49152], P(('row', 'col')), may hold values from -3 to 3
- w_down: bfloat16 [49152, 12288], P(('row', 'col'), 'dep'), may hold values from -0.02734375 to 0.02734375
- bias_down: float32 [12288], P('dep'), may hold values from -3 to 3
- amax_history: float32 [1024], replicated, may hold values from 0.5 to 3
Outputs:
- layer_output: bfloat16 [1024, 12288], P(('row', 'col'), 'dep')
- history_next: float32 [1024], replicated
The draws below stay inside these ranges and needn't reach their ends.
All inputs are finite; a program needn't handle non-finite values.
Results may differ from the reference program's by a relative error of at most 0.0039.
Values may be sent and summed in bfloat16 or wider, within the bound.
No kernel may reach another device: no remote copies, remote signals or barrier semaphores. Data moves between devices by JAX's collectives and lax.ppermute only.
A program may use at most 64 MiB of HBM per device.

```python
import math
import jax
import jax.numpy as jnp

D = 12288
FF = 49152
HIST = 1024
TOKENS = 1024


def draw_tokens(key, part):
    key = jax.random.fold_in(key, 11)
    normal_key, jitter_key = jax.random.split(key)
    values = jnp.clip(jax.random.normal(normal_key, (TOKENS, D), jnp.float32), -6.0, 6.0)
    jitter = jnp.exp(jax.random.uniform(jitter_key, (TOKENS, 1), jnp.float32, math.log(0.7), math.log(1.4)))
    position = jnp.arange(TOKENS, dtype=jnp.float32)[:, None] / max(TOKENS - 1, 1)
    rising = (1.0 + 2.0 * position) / 2.0
    return (values * rising * jitter).astype(jnp.bfloat16)


def draw_w_up(key, part):
    key = jax.random.fold_in(key, 23)
    normal_key, jitter_key = jax.random.split(key)
    values = jnp.clip(jax.random.normal(normal_key, (D, FF), jnp.float32), -6.0, 6.0)
    jitter = jnp.exp(jax.random.uniform(jitter_key, (1, FF), jnp.float32, math.log(0.7), math.log(1.4)))
    position = jnp.arange(FF, dtype=jnp.float32)[None, :] / max(FF - 1, 1)
    rising = (1.0 + 2.0 * position) / 2.0
    return (values * rising * jitter / math.sqrt(D)).astype(jnp.bfloat16)


def draw_amax_history(key, part):
    key = jax.random.fold_in(key, 37)
    lower, upper = (0.5, 2.0)
    logs = jax.random.uniform(key, (HIST,), jnp.float32, math.log(lower), math.log(upper))
    return jnp.exp(logs).astype(jnp.float32)


def levels(stream_key, shape, shards, smallest, top_value):
    def one(axis_at, parts):
        steps = jax.random.uniform(jax.random.fold_in(jax.random.fold_in(stream_key, 6), axis_at), (parts,), jnp.float32, smallest / len(shards), top_value / len(shards))
        return jnp.repeat(jnp.exp(steps), shape[axis_at] // parts).reshape((-1,) + (1,) * (len(shape) - axis_at - 1))

    gain = one(*shards[0])
    for cut in shards[1:]:
        gain = gain * one(*cut)
    return gain


def normal_values(stream_key, dims, deviation, bound, cuts=(), held_as=jnp.bfloat16):
    drawn = deviation * jax.random.normal(stream_key, dims, jnp.float32)
    if cuts:
        drawn = drawn * levels(stream_key, dims, cuts, -0.22, 0.18)
    return jnp.clip(drawn, -bound, bound).astype(held_as)


def setup_inputs(seed: int = 0) -> dict:
    keys = jax.random.split(jax.random.key(seed), 7)
    return {
        "tokens": draw_tokens(jax.random.fold_in(keys[6], 71), 0),
        "w_up": draw_w_up(jax.random.fold_in(keys[6], 71), 0),
        "bias_up": normal_values(keys[2], (FF,), 0.5, 3.0, ((0, 32),), jnp.float32),
        "w_down": normal_values(keys[3], (FF, D), FF ** -0.5, 0.02734375, ((0, 32), (1, 8))),
        "bias_down": normal_values(keys[4], (D,), 0.5, 3.0, ((0, 8),), jnp.float32),
        "amax_history": draw_amax_history(jax.random.fold_in(keys[6], 71), 0),
    }


format_limit = 448.0


def reference(tokens, w_up, bias_up, w_down, bias_down, amax_history):
    scale_factor = format_limit / jnp.max(amax_history)
    pre_activation = jnp.dot(tokens, w_up, preferred_element_type=jnp.float32) + bias_up[None, :]
    activated = jax.nn.gelu(pre_activation, approximate=True)
    new_peak = jnp.max(jnp.abs(activated))
    quantized = jnp.clip(activated * scale_factor, -format_limit, format_limit).astype(jnp.bfloat16)
    summed = jnp.dot(quantized, w_down, preferred_element_type=jnp.float32)
    layer_output = (summed / scale_factor + bias_down[None, :]).astype(jnp.bfloat16)
    history_next = jnp.concatenate([new_peak.reshape(1), amax_history[:-1]])
    return layer_output, history_next
```

```python
import jax
import jax.numpy as jnp
from jax import lax
from jax.sharding import PartitionSpec as P

format_limit = 448.0
f32, f16, bf16 = jnp.float32, jnp.float16, jnp.bfloat16

up_gain = 16.0
down_gain = 64.0

core_swap = [(0, 1), (1, 0), (2, 3), (3, 2)]
x_hi_swap = [(0, 2), (2, 0), (1, 3), (3, 1)]
x_lo_swap = [(i, (i + 4) % 8) for i in range(8)]
y_up = [(4 * l + i, 4 * l + (i + 1) % 4) for l in range(2) for i in range(4)]
y_down = [(4 * l + (i + 1) % 4, 4 * l + i) for l in range(2) for i in range(4)]


def dot(a, b):
    return jnp.dot(a, b, preferred_element_type=f32)


def gather_tokens(tokens):
    pair = jnp.concatenate([tokens, lax.ppermute(tokens, "col", x_hi_swap)])
    mine = lax.all_gather(pair, "row", axis=0, tiled=True)
    return mine, lax.ppermute(mine, "col", core_swap)


def gather_hidden(q):
    n = q.shape[0]
    p = lax.ppermute(q, "dep", x_lo_swap)
    a_q = lax.ppermute(q, "dep", y_up)
    b_q = lax.ppermute(q, "dep", y_down)
    a_p = lax.ppermute(p, "dep", y_up)
    b_p = lax.ppermute(p, "dep", y_down)
    h = n // 2
    c = lax.ppermute(jnp.concatenate([a_q[:h], a_p[:h]]), "dep", y_up)
    d = lax.ppermute(jnp.concatenate([b_q[h:], b_p[h:]]), "dep", y_down)
    rel = jnp.stack(
        [
            jnp.stack([q, a_q, jnp.concatenate([c[:h], d[:h]]), b_q]),
            jnp.stack([p, a_p, jnp.concatenate([c[h:], d[h:]]), b_p]),
        ]
    )
    me = lax.axis_index("dep")
    lo, y = me // 4, me % 4
    parts = []
    for l in range(2):
        for k in range(4):
            parts.append(rel[(l + lo) % 2, (y - k) % 4])
    return jnp.concatenate(parts)


def local(tokens, w_up, bias_up, w_down, bias_down, amax_history):
    scale_factor = format_limit / jnp.max(amax_history)
    mine, other = gather_tokens(tokens)
    up = jnp.concatenate([dot(mine, w_up), dot(other, w_up)])
    sent = (up * up_gain).astype(f16)
    got = lax.all_to_all(sent.reshape(8, 128, 1536), "dep", 0, 0, tiled=True)
    summed = jnp.sum(got.astype(f32), axis=0) * (1.0 / up_gain)
    activated = jax.nn.gelu(summed + bias_up[None, :], approximate=True)
    peaks = lax.all_gather(jnp.max(jnp.abs(activated)).reshape(1), ("row", "col", "dep"), axis=0, tiled=True)
    new_peak = jnp.max(peaks)
    quantized = jnp.clip(activated * scale_factor, -format_limit, format_limit).astype(bf16)
    full_rows = gather_hidden(quantized)
    factor = down_gain / scale_factor
    away = (dot(full_rows[512:], w_down) * factor).astype(f16)
    came = lax.ppermute(away, "col", core_swap)
    near = dot(full_rows[:512], w_down) * factor + came.astype(f32)
    near = near.reshape(8, 2, 32, 1536)
    came = lax.ppermute(near[:, 1].astype(f16), "col", x_hi_swap)
    near = near[:, 0] + came.astype(f32)
    got = lax.all_to_all(near.astype(f16), "row", 0, 0, tiled=True)
    mixed = jnp.sum(got.astype(f32), axis=0) * (1.0 / down_gain)
    layer_output = (mixed + bias_down[None, :]).astype(bf16)
    history_next = jnp.concatenate([new_peak.reshape(1), amax_history[:-1]])
    return (layer_output, history_next)


def solution(mesh):
    in_specs = (
        P(("row", "col"), "dep"),
        P("dep", ("row", "col")),
        P(("row", "col")),
        P(("row", "col"), "dep"),
        P("dep"),
        P(),
    )
    out_specs = (P(("row", "col"), "dep"), P())
    return jax.shard_map(local, mesh=mesh, in_specs=in_specs, out_specs=out_specs, check_vma=False)
```

```python
import jax
import jax.numpy as jnp
from jax import lax
from jax.sharding import PartitionSpec as P

format_limit = 448.0
f32, f16, bf16 = jnp.float32, jnp.float16, jnp.bfloat16

up_gain = 16.0
down_gain = 64.0

core_swap = [(0, 1), (1, 0), (2, 3), (3, 2)]
x_hi_swap = [(0, 2), (2, 0), (1, 3), (3, 1)]
x_lo_swap = [(i, (i + 4) % 8) for i in range(8)]


def dot(a, b):
    return jnp.dot(a, b, preferred_element_type=f32)


def from_z(x, k):
    return lax.ppermute(x, "row", [((i + k) % 8, i) for i in range(8)])


def from_y(x, k):
    return lax.ppermute(x, "dep", [(4 * l + (i + k) % 4, 4 * l + i) for l in range(2) for i in range(4)])


def after(x, y):
    return lax.optimization_barrier((x, y))[0]


def gather_tokens(tokens):
    n, width = tokens.shape[0] // 2, tokens.shape[1]
    came = lax.ppermute(tokens, "col", x_hi_swap)
    own = jnp.concatenate([tokens[:n], came[:n], tokens[n:], came[n:]])
    z1, z7, z2, z6 = from_z(own, 1), from_z(own, 7), from_z(own, 2), from_z(own, 6)
    z3, z5 = from_z(z2, 1), from_z(z6, 7)
    z4 = jnp.concatenate([from_z(z2[: 2 * n], 2), from_z(z6[2 * n :], 6)])
    mine = jnp.stack([own, z1, z2, z3, z4, z5, z6, z7])
    both = jnp.stack([mine, lax.ppermute(mine, "col", core_swap)])
    both = both.reshape(2, 4, 2, 2, 2 * n, width)
    return both.transpose(3, 1, 0, 2, 4, 5).reshape(64 * n, width)


def local(tokens, w_up, bias_up, w_down, bias_down, amax_history):
    scale_factor = format_limit / jnp.max(amax_history)
    factor = down_gain / scale_factor
    dep, z = lax.axis_index("dep"), lax.axis_index("row")
    lo, y = dep // 4, dep % 4
    turn = (24 - z - 2 * y) % 8
    n, width = tokens.shape[0] // 2, tokens.shape[1]

    rows = gather_tokens(tokens)
    sent = (dot(rows, w_up) * up_gain).astype(f16).reshape(8, 8 * n, -1)
    got = lax.all_to_all(sent, "dep", 0, 0, tiled=True)
    summed = jnp.sum(got.astype(f32), axis=0) * (1.0 / up_gain)
    activated = jax.nn.gelu(summed + bias_up[None, :], approximate=True)
    peak = jnp.full((256, 128), jnp.max(jnp.abs(activated)))
    peak = lax.all_to_all(peak, ("row", "col", "dep"), 0, 0, tiled=True)
    q = jnp.clip(activated * scale_factor, -format_limit, format_limit).astype(bf16)

    h = 4 * n
    q1, q3 = from_y(q, 1), from_y(q, 3)
    p = lax.ppermute(q, "dep", x_lo_swap)
    q2 = from_y(q1[:h], 1), from_y(q3[h:], 3)
    p1, p3 = from_y(p, 1), from_y(p, 3)
    p2 = from_y(p1[:h], 1), from_y(p3[h:], 3)
    families = [
        [jnp.concatenate([v0[s], v1[s], v2[i], v3[s]]) for i, s in enumerate((slice(0, h), slice(h, 2 * h)))]
        for v0, v1, v2, v3 in ((q, q1, q2, q3), (p, p1, p2, p3))
    ]

    def away(rows):
        return lax.ppermute((dot(rows[1], w_down) * factor).astype(f16), "col", core_swap)

    def near(rows, came):
        total = (dot(rows[0], w_down) * factor + came.astype(f32)).reshape(8, 2, n, -1)
        return total[:, 0], total[:, 1].astype(f16)

    def turned(keep, came):
        total = (keep + came.astype(f32)).astype(f16)
        return lax.dynamic_slice_in_dim(jnp.concatenate([total, total]), turn, 8)

    def over_x_hi(x):
        return lax.ppermute(x, "col", x_hi_swap)

    def over_row(x):
        return lax.all_to_all(x, "row", 0, 0, tiled=True)

    def finish(got):
        mixed = jnp.sum(got.astype(f32), axis=0) * (1.0 / down_gain)
        return (mixed + bias_down[None, :]).astype(bf16)

    q_rows, p_rows = families
    q_came = away(q_rows)
    q_keep, q_send = near(q_rows, q_came)
    p_rows, peak = after((p_rows, peak), q_send)
    q_got = over_row(turned(q_keep, over_x_hi(q_send)))
    p_came = away(p_rows)
    p_keep, p_send = near(p_rows, p_came)
    p_got = over_row(after(turned(p_keep, over_x_hi(p_send)), q_got))
    q_out, p_out = finish(q_got), finish(p_got)
    first = lo == 0
    layer_output = jnp.concatenate([jnp.where(first, q_out, p_out), jnp.where(first, p_out, q_out)])
    history_next = jnp.concatenate([jnp.max(peak).reshape(1), amax_history[:-1]])
    return (layer_output, history_next)


def solution(mesh):
    in_specs = (
        P(("row", "col"), "dep"),
        P("dep", ("row", "col")),
        P(("row", "col")),
        P(("row", "col"), "dep"),
        P("dep"),
        P(),
    )
    out_specs = (P(("row", "col"), "dep"), P())
    return jax.shard_map(local, mesh=mesh, in_specs=in_specs, out_specs=out_specs, check_vma=False)
```

```python
import jax
import jax.numpy as jnp
from jax import lax
from jax.sharding import PartitionSpec as P

format_limit = 448.0
f32, f16, bf16 = jnp.float32, jnp.float16, jnp.bfloat16

up_gain = 16.0
down_gain = 64.0

core_swap = [(0, 1), (1, 0), (2, 3), (3, 2)]
x_hi_swap = [(0, 2), (2, 0), (1, 3), (3, 1)]
x_lo_swap = [(i, (i + 4) % 8) for i in range(8)]


def dot(a, b):
    return jnp.dot(a, b, preferred_element_type=f32)


def from_z(x, k):
    return lax.ppermute(x, "row", [((i + k) % 8, i) for i in range(8)])


def from_y(x, k):
    return lax.ppermute(x, "dep", [(4 * l + (i + k) % 4, 4 * l + i) for l in range(2) for i in range(4)])


def after(x, y):
    return lax.optimization_barrier((x, y))[0]


def gather_tokens(tokens):
    n, width = tokens.shape[0] // 2, tokens.shape[1]
    came = lax.ppermute(tokens, "col", x_hi_swap)
    own = jnp.concatenate([tokens[:n], came[:n], tokens[n:], came[n:]])
    z1, z7, z2, z6 = from_z(own, 1), from_z(own, 7), from_z(own, 2), from_z(own, 6)
    z3, z5 = from_z(z2, 1), from_z(z6, 7)
    z4 = jnp.concatenate([from_z(z2[: 2 * n], 2), from_z(z6[2 * n :], 6)])
    mine = jnp.stack([own, z1, z2, z3, z4, z5, z6, z7])
    both = jnp.stack([mine, lax.ppermute(mine, "col", core_swap)])
    both = both.reshape(2, 4, 2, 2, 2 * n, width)
    return both.transpose(3, 1, 0, 2, 4, 5).reshape(64 * n, width)


def peak_over(peak, *steps):
    for axis, step in steps:
        size = {"row": 8, "col": 4, "dep": 8}[axis]
        peak = jnp.maximum(peak, lax.ppermute(peak, axis, [(i, i ^ step) for i in range(size)]))
    return peak


def local(tokens, w_up, bias_up, w_down, bias_down, amax_history):
    scale_factor = format_limit / jnp.max(amax_history)
    factor = down_gain / scale_factor
    dep, z = lax.axis_index("dep"), lax.axis_index("row")
    lo, y = dep // 4, dep % 4
    turn = (24 - z - 2 * y) % 8
    n, width = tokens.shape[0] // 2, tokens.shape[1]

    rows = gather_tokens(tokens)
    sent = (dot(rows, w_up) * up_gain).astype(f16).reshape(8, 8 * n, -1)
    got = lax.all_to_all(sent, "dep", 0, 0, tiled=True)
    summed = jnp.sum(got.astype(f32), axis=0) * (1.0 / up_gain)
    activated = jax.nn.gelu(summed + bias_up[None, :], approximate=True)
    peak = jnp.full((8, 128), jnp.max(jnp.abs(activated)))
    q = jnp.clip(activated * scale_factor, -format_limit, format_limit).astype(bf16)

    h = 4 * n
    q1, q3 = from_y(q, 1), from_y(q, 3)
    p = lax.ppermute(q, "dep", x_lo_swap)
    peak, q1, q3 = lax.optimization_barrier((peak_over(peak, ("row", 1), ("row", 2)), q1, q3))
    q2 = from_y(q1[:h], 1), from_y(q3[h:], 3)
    p1, p3 = from_y(p, 1), from_y(p, 3)
    p2 = from_y(p1[:h], 1), from_y(p3[h:], 3)

    def down(v0, v1, v2, v3, s):
        return dot(jnp.concatenate([v0[s], v1[s], v2[s.start // h], v3[s]]), w_down) * factor

    own_core, other_core = slice(0, h), slice(h, 2 * h)

    def over_core(total):
        return lax.ppermute(total.astype(f16), "col", core_swap)

    def near(total, came):
        total = (total + came.astype(f32)).reshape(8, 2, n, -1)
        return total[:, 0], total[:, 1].astype(f16)

    def turned(keep, came):
        total = (keep + came.astype(f32)).astype(f16)
        return lax.dynamic_slice_in_dim(jnp.concatenate([total, total]), turn, 8)

    def over_x_hi(x):
        return lax.ppermute(x, "col", x_hi_swap)

    def over_row(x):
        return lax.all_to_all(x, "row", 0, 0, tiled=True)

    def finish(got):
        mixed = jnp.sum(got.astype(f32), axis=0) * (1.0 / down_gain)
        return (mixed + bias_down[None, :]).astype(bf16)

    q_came = over_core(down(q, q1, q2, q3, other_core))
    q_keep, q_send = near(down(q, q1, q2, q3, own_core), q_came)
    p2 = after(p2, q_send)
    p_came = over_core(down(p, p1, p2, p3, other_core))
    p_total = down(p, p1, p2, p3, own_core)
    q_sum = turned(q_keep, over_x_hi(q_send))
    q_got = over_row(q_sum)
    peak = peak_over(peak, ("row", 4), ("col", 1))
    p_total, p_came, peak = after((p_total, p_came, peak), q_sum)
    p_keep, p_send = near(p_total, p_came)
    p_came, peak = lax.optimization_barrier((over_x_hi(p_send), peak))
    peak = peak_over(peak, ("dep", 1), ("dep", 2))
    p_sum, peak = after((turned(p_keep, p_came), peak), q_got)
    p_got = over_row(p_sum)
    peak = peak_over(peak, ("dep", 4), ("col", 2))
    q_out, p_out = finish(q_got), finish(p_got)
    first = lo == 0
    layer_output = jnp.concatenate([jnp.where(first, q_out, p_out), jnp.where(first, p_out, q_out)])
    history_next = jnp.concatenate([peak[0, :1], amax_history[:-1]])
    return (layer_output, history_next)


def solution(mesh):
    in_specs = (
        P(("row", "col"), "dep"),
        P("dep", ("row", "col")),
        P(("row", "col")),
        P(("row", "col"), "dep"),
        P("dep"),
        P(),
    )
    out_specs = (P(("row", "col"), "dep"), P())
    return jax.shard_map(local, mesh=mesh, in_specs=in_specs, out_specs=out_specs, check_vma=False)
```

```python
import jax
import jax.numpy as jnp
from jax import lax
from jax.sharding import PartitionSpec as P

format_limit = 448.0
f32, f16, bf16 = jnp.float32, jnp.float16, jnp.bfloat16

up_gain = 16.0
down_gain = 64.0

core_swap = [(0, 1), (1, 0), (2, 3), (3, 2)]
x_hi_swap = [(0, 2), (2, 0), (1, 3), (3, 1)]
x_lo_swap = [(i, (i + 4) % 8) for i in range(8)]


def dot(a, b):
    return jnp.dot(a, b, preferred_element_type=f32)


def from_z(x, k):
    return lax.ppermute(x, "row", [((i + k) % 8, i) for i in range(8)])


def from_y(x, k):
    return lax.ppermute(x, "dep", [(4 * l + (i + k) % 4, 4 * l + i) for l in range(2) for i in range(4)])


def after(x, y):
    return lax.optimization_barrier((x, y))[0]


def gather_tokens(tokens):
    n, width = tokens.shape[0] // 2, tokens.shape[1]
    came = lax.ppermute(tokens, "col", x_hi_swap)
    own = jnp.concatenate([tokens[:n], came[:n], tokens[n:], came[n:]])
    z1, z7, z2, z6 = from_z(own, 1), from_z(own, 7), from_z(own, 2), from_z(own, 6)
    z3, z5 = from_z(z2, 1), from_z(z6, 7)
    z4 = jnp.concatenate([from_z(z2[: 2 * n], 2), from_z(z6[2 * n :], 6)])
    mine = jnp.stack([own, z1, z2, z3, z4, z5, z6, z7])
    both = jnp.stack([mine, lax.ppermute(mine, "col", core_swap)])
    both = both.reshape(2, 4, 2, 2, 2 * n, width)
    return both.transpose(3, 1, 0, 2, 4, 5).reshape(64 * n, width)


def peak_over(peak, *steps):
    for axis, step in steps:
        size = {"row": 8, "col": 4, "dep": 8}[axis]
        peak = jnp.maximum(peak, lax.ppermute(peak, axis, [(i, i ^ step) for i in range(size)]))
    return peak


def local(tokens, w_up, bias_up, w_down, bias_down, amax_history):
    scale_factor = format_limit / jnp.max(amax_history)
    factor = down_gain / scale_factor
    dep, z = lax.axis_index("dep"), lax.axis_index("row")
    lo, y = dep // 4, dep % 4
    turn = (24 - z - 2 * y) % 8
    n, width = tokens.shape[0] // 2, tokens.shape[1]

    rows = gather_tokens(tokens)
    half, own_lo = w_up.shape[1] // 2, lo == 0

    def up(w):
        return (dot(rows, w) * up_gain).reshape(2, 4, 8 * n, -1)

    def over_x_lo(x):
        came = lax.ppermute(jnp.where(own_lo, x[1], x[0]).astype(f16), "dep", x_lo_swap)
        return jnp.where(own_lo, x[0], x[1]) + came.astype(f32)

    b_sent = up(w_up[:, half:]).astype(f16).transpose(1, 0, 2, 3)
    b_got = lax.all_to_all(b_sent, "dep", 0, 0, tiled=True, axis_index_groups=[[0, 1, 2, 3], [4, 5, 6, 7]])
    a_sum = over_x_lo(up(w_up[:, :half]))
    a_sum = lax.dynamic_slice_in_dim(jnp.concatenate([a_sum, a_sum]), y, 4)
    a_sent = a_sum.astype(f16)
    a_got = [from_y(a_sent[j], 4 - j).astype(f32) for j in (1, 2, 3)]
    b_sum = over_x_lo(jnp.sum(b_got.astype(f32), axis=0))
    a_sum = a_sum[0] + a_got[0] + a_got[1] + a_got[2]
    summed = jnp.concatenate([a_sum, b_sum], axis=1) * (1.0 / up_gain)
    activated = jax.nn.gelu(summed + bias_up[None, :], approximate=True)
    peak = jnp.full((8, 128), jnp.max(jnp.abs(activated)))
    q = jnp.clip(activated * scale_factor, -format_limit, format_limit).astype(bf16)

    h = 4 * n
    q1, q3 = from_y(q, 1), from_y(q, 3)
    p = lax.ppermute(q, "dep", x_lo_swap)
    peak, q1, q3 = lax.optimization_barrier((peak_over(peak, ("row", 1), ("row", 2)), q1, q3))
    q2 = lax.optimization_barrier((from_y(q1[:h], 1), from_y(q3[h:], 3)))
    p1, p3 = from_y(p, 1), from_y(p, 3)

    def down(v0, v1, v2, v3, s):
        return dot(jnp.concatenate([v0[s], v1[s], v2[s.start // h], v3[s]]), w_down) * factor

    own_core, other_core = slice(0, h), slice(h, 2 * h)

    def over_core(total):
        return lax.ppermute(total.astype(f16), "col", core_swap)

    def near(total, came):
        total = (total + came.astype(f32)).reshape(8, 2, n, -1)
        return total[:, 0], total[:, 1].astype(f16)

    def turned(keep, came):
        total = (keep + came.astype(f32)).astype(f16)
        return lax.dynamic_slice_in_dim(jnp.concatenate([total, total]), turn, 8)

    def over_x_hi(x):
        return lax.ppermute(x, "col", x_hi_swap)

    def over_row(x):
        return lax.all_to_all(x, "row", 0, 0, tiled=True)

    def finish(got):
        mixed = jnp.sum(got.astype(f32), axis=0) * (1.0 / down_gain)
        return (mixed + bias_down[None, :]).astype(bf16)

    q_came = over_core(down(q, q1, q2, q3, other_core))
    q_keep, q_send = near(down(q, q1, q2, q3, own_core), q_came)
    p2_low, p2_high, peak = after((p1[:h], p3[h:], peak), q_send)
    p2 = from_y(p2_low, 1), from_y(p2_high, 3)
    p_came = over_core(down(p, p1, p2, p3, other_core))
    p_total = down(p, p1, p2, p3, own_core)
    q_sum = turned(q_keep, over_x_hi(q_send))
    q_got = over_row(q_sum)
    peak = peak_over(peak, ("row", 4))
    p_total, p_came, peak = after((p_total, p_came, peak), q_sum)
    p_keep, p_send = near(p_total, p_came)
    p_came, peak = lax.optimization_barrier((over_x_hi(p_send), peak))
    peak = peak_over(peak, ("dep", 1), ("dep", 2))
    p_sum, peak = after((turned(p_keep, p_came), peak), q_got)
    p_got = over_row(p_sum)
    peak = peak_over(peak, ("dep", 4), ("col", 1), ("col", 2))
    q_out, p_out = finish(q_got), finish(p_got)
    first = lo == 0
    layer_output = jnp.concatenate([jnp.where(first, q_out, p_out), jnp.where(first, p_out, q_out)])
    history_next = jnp.concatenate([peak[0, :1], amax_history[:-1]])
    return (layer_output, history_next)


def solution(mesh):
    in_specs = (
        P(("row", "col"), "dep"),
        P("dep", ("row", "col")),
        P(("row", "col")),
        P(("row", "col"), "dep"),
        P("dep"),
        P(),
    )
    out_specs = (P(("row", "col"), "dep"), P())
    return jax.shard_map(local, mesh=mesh, in_specs=in_specs, out_specs=out_specs, check_vma=False)
```

```python
import jax
import jax.numpy as jnp
from jax import lax
from jax.sharding import PartitionSpec as P

format_limit = 448.0
f32, f16, bf16 = jnp.float32, jnp.float16, jnp.bfloat16

up_gain = 16.0
down_gain = 64.0

core_swap = [(0, 1), (1, 0), (2, 3), (3, 2)]
x_hi_swap = [(0, 2), (2, 0), (1, 3), (3, 1)]
x_lo_swap = [(i, (i + 4) % 8) for i in range(8)]


def dot(a, b):
    return jnp.dot(a, b, preferred_element_type=f32)


def from_z(x, k):
    return lax.ppermute(x, "row", [((i + k) % 8, i) for i in range(8)])


def from_y(x, k):
    return lax.ppermute(x, "dep", [(4 * l + (i + k) % 4, 4 * l + i) for l in range(2) for i in range(4)])


def after(x, y):
    return lax.optimization_barrier((x, y))[0]


def gather_tokens(tokens):
    n, width = tokens.shape[0] // 2, tokens.shape[1]
    came = lax.ppermute(tokens, "col", x_hi_swap)
    own = jnp.concatenate([tokens[:n], came[:n], tokens[n:], came[n:]])
    z1, z7, z2, z6 = from_z(own, 1), from_z(own, 7), from_z(own, 2), from_z(own, 6)
    z3, z5 = from_z(z2, 1), from_z(z6, 7)
    z4 = jnp.concatenate([from_z(z2[: 2 * n], 2), from_z(z6[2 * n :], 6)])
    mine = jnp.stack([own, z1, z2, z3, z4, z5, z6, z7])
    both = jnp.stack([mine, lax.ppermute(mine, "col", core_swap)])
    both = both.reshape(2, 4, 2, 2, 2 * n, width)
    return both.transpose(1, 3, 0, 2, 4, 5).reshape(64 * n, width)


def peak_over(peak, *steps):
    for axis, step in steps:
        size = {"row": 8, "col": 4, "dep": 8}[axis]
        peak = jnp.maximum(peak, lax.ppermute(peak, axis, [(i, i ^ step) for i in range(size)]))
    return peak


def local(tokens, w_up, bias_up, w_down, bias_down, amax_history):
    scale_factor = format_limit / jnp.max(amax_history)
    factor = down_gain / scale_factor
    dep, z = lax.axis_index("dep"), lax.axis_index("row")
    lo, y = dep // 4, dep % 4
    turn = (24 - z - 2 * y) % 8
    n, width = tokens.shape[0] // 2, tokens.shape[1]

    rows = gather_tokens(tokens)
    half, own_lo = w_up.shape[1] // 2, lo == 0

    def up(w):
        return (dot(rows, w) * up_gain).reshape(4, 2, 8 * n, -1)

    def over_x_lo(x):
        x0, x1 = x[..., 0, :, :], x[..., 1, :, :]
        came = lax.ppermute(jnp.where(own_lo, x1, x0).astype(f16), "dep", x_lo_swap)
        return jnp.where(own_lo, x0, x1) + came.astype(f32)

    b_sent = up(w_up[:, half:]).astype(f16)
    b_got = lax.all_to_all(b_sent, "dep", 0, 0, tiled=True, axis_index_groups=[[0, 1, 2, 3], [4, 5, 6, 7]])
    a_sum = over_x_lo(up(w_up[:, :half]))
    a_sum = lax.dynamic_slice_in_dim(jnp.concatenate([a_sum, a_sum]), y, 4)
    a_sent = a_sum.astype(f16)
    a_got = [from_y(a_sent[j], 4 - j).astype(f32) for j in (1, 2, 3)]
    b_sum = over_x_lo(jnp.sum(b_got.astype(f32), axis=0))
    a_sum = a_sum[0] + a_got[0] + a_got[1] + a_got[2]
    summed = jnp.concatenate([a_sum, b_sum], axis=1) * (1.0 / up_gain)
    activated = jax.nn.gelu(summed + bias_up[None, :], approximate=True)
    peak = jnp.full((8, 128), jnp.max(jnp.abs(activated)))
    q = jnp.clip(activated * scale_factor, -format_limit, format_limit).astype(bf16)

    h = 4 * n
    q1, q3 = from_y(q, 1), from_y(q, 3)
    p = lax.ppermute(q, "dep", x_lo_swap)
    peak, q1, q3 = lax.optimization_barrier((peak_over(peak, ("row", 1), ("row", 2)), q1, q3))
    q2 = lax.optimization_barrier((from_y(q1[:h], 1), from_y(q3[h:], 3)))
    p1, p3 = from_y(p, 1), from_y(p, 3)

    def down(v0, v1, v2, v3, s):
        return dot(jnp.concatenate([v0[s], v1[s], v2[s.start // h], v3[s]]), w_down) * factor

    own_core, other_core = slice(0, h), slice(h, 2 * h)

    def over_core(total):
        return lax.ppermute(total.astype(f16), "col", core_swap)

    def near(total, came):
        total = (total + came.astype(f32)).reshape(8, 2, n, -1)
        return total[:, 0], total[:, 1].astype(f16)

    def turned(keep, came):
        total = (keep + came.astype(f32)).astype(f16)
        return lax.dynamic_slice_in_dim(jnp.concatenate([total, total]), turn, 8)

    def over_x_hi(x):
        return lax.ppermute(x, "col", x_hi_swap)

    def over_row(x):
        return lax.all_to_all(x, "row", 0, 0, tiled=True)

    def finish(got):
        mixed = jnp.sum(got.astype(f32), axis=0) * (1.0 / down_gain)
        return (mixed + bias_down[None, :]).astype(bf16)

    q_came = over_core(down(q, q1, q2, q3, other_core))
    q_keep, q_send = near(down(q, q1, q2, q3, own_core), q_came)
    p2_low, p2_high, peak = after((p1[:h], p3[h:], peak), q_send)
    p2 = from_y(p2_low, 1), from_y(p2_high, 3)
    p_came = over_core(down(p, p1, p2, p3, other_core))
    p_total = down(p, p1, p2, p3, own_core)
    q_sum = turned(q_keep, over_x_hi(q_send))
    q_got = over_row(q_sum)
    peak = peak_over(peak, ("row", 4))
    p_total, p_came, peak = after((p_total, p_came, peak), q_sum)
    p_keep, p_send = near(p_total, p_came)
    p_came, peak = lax.optimization_barrier((over_x_hi(p_send), peak))
    peak = peak_over(peak, ("dep", 1), ("dep", 2))
    p_sum, peak = after((turned(p_keep, p_came), peak), q_got)
    p_got = over_row(p_sum)
    peak = peak_over(peak, ("dep", 4), ("col", 1), ("col", 2))
    q_out, p_out = finish(q_got), finish(p_got)
    first = lo == 0
    layer_output = jnp.concatenate([jnp.where(first, q_out, p_out), jnp.where(first, p_out, q_out)])
    history_next = jnp.concatenate([peak[0, :1], amax_history[:-1]])
    return (layer_output, history_next)


def solution(mesh):
    in_specs = (
        P(("row", "col"), "dep"),
        P("dep", ("row", "col")),
        P(("row", "col")),
        P(("row", "col"), "dep"),
        P("dep"),
        P(),
    )
    out_specs = (P(("row", "col"), "dep"), P())
    return jax.shard_map(local, mesh=mesh, in_specs=in_specs, out_specs=out_specs, check_vma=False)
```

```python
import jax
import jax.numpy as jnp
from jax import lax
from jax.sharding import PartitionSpec as P

format_limit = 448.0
f32, f16, bf16 = jnp.float32, jnp.float16, jnp.bfloat16

up_gain = 16.0
down_gain = 64.0

core_swap = [(0, 1), (1, 0), (2, 3), (3, 2)]
x_hi_swap = [(0, 2), (2, 0), (1, 3), (3, 1)]
x_lo_swap = [(i, (i + 4) % 8) for i in range(8)]


def dot(a, b):
    return jnp.dot(a, b, preferred_element_type=f32)


def from_z(x, k):
    return lax.ppermute(x, "row", [((i + k) % 8, i) for i in range(8)])


def from_y(x, k):
    return lax.ppermute(x, "dep", [(4 * l + (i + k) % 4, 4 * l + i) for l in range(2) for i in range(4)])


def after(x, y):
    return lax.optimization_barrier((x, y))[0]


def gather_tokens(tokens):
    n, width = tokens.shape[0] // 2, tokens.shape[1]
    came = lax.ppermute(tokens, "col", x_hi_swap)
    own = jnp.concatenate([tokens[:n], came[:n], tokens[n:], came[n:]])
    z1, z7, z2, z6 = from_z(own, 1), from_z(own, 7), from_z(own, 2), from_z(own, 6)
    z3, z5 = from_z(z2, 1), from_z(z6, 7)
    z4 = jnp.concatenate([from_z(z2[: 2 * n], 2), from_z(z6[2 * n :], 6)])
    mine = jnp.stack([own, z1, z2, z3, z4, z5, z6, z7])
    both = jnp.stack([mine, lax.ppermute(mine, "col", core_swap)])
    both = both.reshape(2, 4, 2, 2, 2 * n, width)
    return both.transpose(1, 3, 0, 2, 4, 5).reshape(64 * n, width)


def peak_over(peak, *steps):
    for axis, step in steps:
        size = {"row": 8, "col": 4, "dep": 8}[axis]
        peak = jnp.maximum(peak, lax.ppermute(peak, axis, [(i, i ^ step) for i in range(size)]))
    return peak


def local(tokens, w_up, bias_up, w_down, bias_down, amax_history):
    scale_factor = format_limit / jnp.max(amax_history)
    factor = down_gain / scale_factor
    dep, z = lax.axis_index("dep"), lax.axis_index("row")
    lo, y = dep // 4, dep % 4
    turn = (24 - z - 2 * y) % 8
    n, width = tokens.shape[0] // 2, tokens.shape[1]

    rows = gather_tokens(tokens)
    half, own_lo = w_up.shape[1] // 2, lo == 0

    def up(w):
        return (dot(rows, w) * up_gain).reshape(4, 2, 8 * n, -1)

    def over_x_lo(x):
        x0, x1 = x[..., 0, :, :], x[..., 1, :, :]
        came = lax.ppermute(jnp.where(own_lo, x1, x0).astype(f16), "dep", x_lo_swap)
        return jnp.where(own_lo, x0, x1) + came.astype(f32)

    b_sent = up(w_up[:, half:]).astype(f16)
    b_got = lax.all_to_all(b_sent, "dep", 0, 0, tiled=True, axis_index_groups=[[0, 1, 2, 3], [4, 5, 6, 7]])
    a_sum = over_x_lo(up(w_up[:, :half]))
    a_sum = lax.dynamic_slice_in_dim(jnp.concatenate([a_sum, a_sum]), y, 4)
    a_sent = a_sum.astype(f16)
    a_got = [from_y(a_sent[j], 4 - j).astype(f32) for j in (1, 2, 3)]
    b_sum = over_x_lo(jnp.sum(b_got.astype(f32), axis=0))
    a_sum = a_sum[0] + a_got[0] + a_got[1] + a_got[2]
    summed = jnp.concatenate([a_sum, b_sum], axis=1) * (1.0 / up_gain)
    activated = jax.nn.gelu(summed + bias_up[None, :], approximate=True)
    peak = jnp.full((8, 128), jnp.max(jnp.abs(activated)))
    q = jnp.clip(activated * scale_factor, -format_limit, format_limit).astype(bf16)

    h = 4 * n
    q1, q3 = from_y(q, 1), from_y(q, 3)
    p = lax.ppermute(q, "dep", x_lo_swap)
    peak, q1, q3 = lax.optimization_barrier((peak_over(peak, ("row", 1), ("row", 2)), q1, q3))
    q2 = lax.optimization_barrier((from_y(q1[:h], 1), from_y(q3[h:], 3)))
    p1, p3 = from_y(p, 1), from_y(p, 3)

    def down(*rows):
        return dot(jnp.concatenate(rows), w_down) * factor

    def over_core(total):
        return lax.ppermute(total.astype(f16), "col", core_swap)

    def near(total, came):
        total = (total + came.astype(f32)).reshape(8, 2, n, -1)
        return total[:, 0], total[:, 1].astype(f16)

    def turned(keep, came):
        total = (keep + came.astype(f32)).astype(f16)
        return lax.dynamic_slice_in_dim(jnp.concatenate([total, total]), turn, 8)

    def over_x_hi(x):
        return lax.ppermute(x, "col", x_hi_swap)

    def over_row(x):
        return lax.all_to_all(x, "row", 0, 0, tiled=True)

    def finish(got):
        mixed = jnp.sum(got.astype(f32), axis=0) * (1.0 / down_gain)
        return (mixed + bias_down[None, :]).astype(bf16)

    q_own = dot(q, w_down) * factor
    q_came = over_core(jnp.concatenate([q_own[h:], down(q1[h:], q2[1], q3[h:])]))
    q_near = jnp.concatenate([q_own[:h], down(q1[:h], q2[0], q3[:h])])
    q_keep, q_send = near(q_near, q_came)
    p2_low, p2_high, peak = after((p1[:h], p3[h:], peak), q_send)
    p2 = from_y(p2_low, 1), from_y(p2_high, 3)
    p_came = over_core(down(p[h:], p1[h:], p2[1], p3[h:]))
    p_total = down(p[:h], p1[:h], p2[0], p3[:h])
    q_sum = turned(q_keep, over_x_hi(q_send))
    q_got = over_row(q_sum)
    peak = peak_over(peak, ("row", 4))
    p_total, p_came, peak = after((p_total, p_came, peak), q_sum)
    p_keep, p_send = near(p_total, p_came)
    p_came, peak = lax.optimization_barrier((over_x_hi(p_send), peak))
    peak = peak_over(peak, ("dep", 1), ("dep", 2))
    p_sum, peak = after((turned(p_keep, p_came), peak), q_got)
    p_got = over_row(p_sum)
    peak = peak_over(peak, ("dep", 4), ("col", 1), ("col", 2))
    q_out, p_out = finish(q_got), finish(p_got)
    first = lo == 0
    layer_output = jnp.concatenate([jnp.where(first, q_out, p_out), jnp.where(first, p_out, q_out)])
    history_next = jnp.concatenate([peak[0, :1], amax_history[:-1]])
    return (layer_output, history_next)


def solution(mesh):
    in_specs = (
        P(("row", "col"), "dep"),
        P("dep", ("row", "col")),
        P(("row", "col")),
        P(("row", "col"), "dep"),
        P("dep"),
        P(),
    )
    out_specs = (P(("row", "col"), "dep"), P())
    return jax.shard_map(local, mesh=mesh, in_specs=in_specs, out_specs=out_specs, check_vma=False)
```

```python
import jax
import jax.numpy as jnp
from jax import lax
from jax.sharding import PartitionSpec as P

format_limit = 448.0
f32, f16, bf16 = jnp.float32, jnp.float16, jnp.bfloat16

up_gain = 16.0
down_gain = 64.0

core_swap = [(0, 1), (1, 0), (2, 3), (3, 2)]
x_hi_swap = [(0, 2), (2, 0), (1, 3), (3, 1)]
x_lo_swap = [(i, (i + 4) % 8) for i in range(8)]


def dot(a, b):
    return jnp.dot(a, b, preferred_element_type=f32)


def from_z(x, k):
    return lax.ppermute(x, "row", [((i + k) % 8, i) for i in range(8)])


def from_y(x, k):
    return lax.ppermute(x, "dep", [(4 * l + (i + k) % 4, 4 * l + i) for l in range(2) for i in range(4)])


def after(x, y):
    return lax.optimization_barrier((x, y))[0]


def gather_tokens(tokens):
    n, width = tokens.shape[0] // 2, tokens.shape[1]
    came = lax.ppermute(tokens, "col", x_hi_swap)
    own = jnp.concatenate([tokens[:n], came[:n], tokens[n:], came[n:]])
    z1, z7, z2, z6 = from_z(own, 1), from_z(own, 7), from_z(own, 2), from_z(own, 6)
    z3, z5 = from_z(z2, 1), from_z(z6, 7)
    z4 = jnp.concatenate([from_z(z2[: 2 * n], 2), from_z(z6[2 * n :], 6)])
    mine = jnp.stack([own, z1, z2, z3, z4, z5, z6, z7])
    def ordered(x):
        return x.reshape(4, 2, 2, 2 * n, width).transpose(0, 2, 1, 3, 4).reshape(32 * n, width)

    return ordered(mine), ordered(lax.ppermute(mine, "col", core_swap))


def peak_over(peak, *steps):
    for axis, step in steps:
        size = {"row": 8, "col": 4, "dep": 8}[axis]
        peak = jnp.maximum(peak, lax.ppermute(peak, axis, [(i, i ^ step) for i in range(size)]))
    return peak


def local(tokens, w_up, bias_up, w_down, bias_down, amax_history):
    scale_factor = format_limit / jnp.max(amax_history)
    factor = down_gain / scale_factor
    dep, z = lax.axis_index("dep"), lax.axis_index("row")
    lo, y = dep // 4, dep % 4
    turn = (24 - z - 2 * y) % 8
    n, width = tokens.shape[0] // 2, tokens.shape[1]

    mine, other = gather_tokens(tokens)
    half, own_lo = w_up.shape[1] // 2, lo == 0

    def up(rows, w):
        return (dot(rows, w) * up_gain).reshape(4, 2, rows.shape[0] // 8, -1)

    def over_x_lo(x):
        x0, x1 = x[..., 0, :, :], x[..., 1, :, :]
        came = lax.ppermute(jnp.where(own_lo, x1, x0).astype(f16), "dep", x_lo_swap)
        return jnp.where(own_lo, x0, x1) + came.astype(f32)

    rows = jnp.concatenate([v.reshape(8, 4 * n, width) for v in (mine, other)], axis=1).reshape(64 * n, width)
    b_sent = up(rows, w_up[:, half:]).astype(f16)
    b_got = lax.all_to_all(b_sent, "dep", 0, 0, tiled=True, axis_index_groups=[[0, 1, 2, 3], [4, 5, 6, 7]])
    a_sum = over_x_lo(jnp.concatenate([up(mine, w_up[:, :half]), up(other, w_up[:, :half])], axis=2))
    a_sum = lax.dynamic_slice_in_dim(jnp.concatenate([a_sum, a_sum]), y, 4)
    a_sent = a_sum.astype(f16)
    a_got = [from_y(a_sent[j], 4 - j).astype(f32) for j in (1, 2, 3)]
    b_sum = over_x_lo(jnp.sum(b_got.astype(f32), axis=0))
    a_sum = a_sum[0] + a_got[0] + a_got[1] + a_got[2]
    summed = jnp.concatenate([a_sum, b_sum], axis=1) * (1.0 / up_gain)
    activated = jax.nn.gelu(summed + bias_up[None, :], approximate=True)
    peak = jnp.full((8, 128), jnp.max(jnp.abs(activated)))
    q = jnp.clip(activated * scale_factor, -format_limit, format_limit).astype(bf16)

    h = 4 * n
    q1, q3 = from_y(q, 1), from_y(q, 3)
    p = lax.ppermute(q, "dep", x_lo_swap)
    peak, q1, q3 = lax.optimization_barrier((peak_over(peak, ("row", 1), ("row", 2)), q1, q3))
    q2 = lax.optimization_barrier((from_y(q1[:h], 1), from_y(q3[h:], 3)))
    p1, p3 = from_y(p, 1), from_y(p, 3)

    def down(*rows):
        return dot(jnp.concatenate(rows), w_down) * factor

    def over_core(total):
        return lax.ppermute(total.astype(f16), "col", core_swap)

    def near(total, came):
        total = (total + came.astype(f32)).reshape(8, 2, n, -1)
        return total[:, 0], total[:, 1].astype(f16)

    def turned(keep, came):
        total = (keep + came.astype(f32)).astype(f16)
        return lax.dynamic_slice_in_dim(jnp.concatenate([total, total]), turn, 8)

    def over_x_hi(x):
        return lax.ppermute(x, "col", x_hi_swap)

    def over_row(x):
        return lax.all_to_all(x, "row", 0, 0, tiled=True)

    def finish(got):
        mixed = jnp.sum(got.astype(f32), axis=0) * (1.0 / down_gain)
        return (mixed + bias_down[None, :]).astype(bf16)

    q_own = dot(q, w_down) * factor
    q_came = over_core(jnp.concatenate([q_own[h:], down(q1[h:], q2[1], q3[h:])]))
    q_near = jnp.concatenate([q_own[:h], down(q1[:h], q2[0], q3[:h])])
    q_keep, q_send = near(q_near, q_came)
    p2_low, p2_high, peak = after((p1[:h], p3[h:], peak), q_send)
    p2 = from_y(p2_low, 1), from_y(p2_high, 3)
    p_came = over_core(down(p[h:], p1[h:], p2[1], p3[h:]))
    p_total = down(p[:h], p1[:h], p2[0], p3[:h])
    q_sum = turned(q_keep, over_x_hi(q_send))
    q_got = over_row(q_sum)
    peak = peak_over(peak, ("row", 4))
    p_total, p_came, peak = after((p_total, p_came, peak), q_sum)
    p_keep, p_send = near(p_total, p_came)
    p_came, peak = lax.optimization_barrier((over_x_hi(p_send), peak))
    peak = peak_over(peak, ("dep", 1), ("dep", 2))
    p_sum, peak = after((turned(p_keep, p_came), peak), q_got)
    p_got = over_row(p_sum)
    peak = peak_over(peak, ("dep", 4), ("col", 1), ("col", 2))
    q_out, p_out = finish(q_got), finish(p_got)
    first = lo == 0
    layer_output = jnp.concatenate([jnp.where(first, q_out, p_out), jnp.where(first, p_out, q_out)])
    history_next = jnp.concatenate([peak[0, :1], amax_history[:-1]])
    return (layer_output, history_next)


def solution(mesh):
    in_specs = (
        P(("row", "col"), "dep"),
        P("dep", ("row", "col")),
        P(("row", "col")),
        P(("row", "col"), "dep"),
        P("dep"),
        P(),
    )
    out_specs = (P(("row", "col"), "dep"), P())
    return jax.shard_map(local, mesh=mesh, in_specs=in_specs, out_specs=out_specs, check_vma=False)
```
